256 devices in a mesh: band: 64 (over x_hi, y, z), pair: 4 (over x_lo, core).
Axes of the slice: x: 4 (x_hi: 2, x_lo: 2; x = x_hi * 2 + x_lo), y: 4, z: 8, core: 2. Of those that a mesh axis runs over, the one named last changes fastest.
Arguments:
- orbitals: float32 [512, 64, 4096], P('band', 'pair'), may hold values from -6 to 6
- pair_table: int32 [8, 2], replicated, may hold values from 0 to 7, as said below
- partner_offset: int32 [1], replicated, may hold values from 1 to 63
Outputs:
- exchange_field: float32 [512, 64, 4096], P('band', 'pair')
- gram: float32 [512, 8], P('band')
The draws below stay inside these ranges and needn't reach their ends.
Inputs may be any that keep to these rules, and one draw needn't show every extreme that they name: In each column of pair_table every band 0 to 7 appears at least once.
All inputs are finite; a program needn't handle non-finite values.
Results may differ from the reference program's by a relative error of at most 0.0052.
Values may be sent and summed in bfloat16 or wider, within the bound.
No kernel may reach another device: no remote copies, remote signals or barrier semaphores. Data moves between devices by JAX's collectives and lax.ppermute only.
A program may use at most 128 MiB of HBM per device.

```python
import math
import jax
import jax.numpy as jnp
from jax import lax

GX = 64
GY = 64
GZ = 64
BLK = 8
PAIRS = 8
GYZ = 4096
NORB = 512
N_BAND = 64


def draw_pair_table(key, part):
    key = jax.random.fold_in(key, 5)
    keys = jax.random.split(key, 6)

    def column(key_cover, key_rest, key_order):
        cover = jax.random.permutation(key_cover, BLK).astype(jnp.int32)
        others = jax.random.randint(key_rest, (PAIRS - BLK,), 0, BLK).astype(jnp.int32)
        joined = jnp.concatenate([cover, others])
        order = jax.random.permutation(key_order, PAIRS).astype(jnp.int32)
        return joined[order]
    first_band = column(keys[0], keys[1], keys[2])
    second_band = column(keys[3], keys[4], keys[5])
    return jnp.stack([first_band, second_band], axis=1).astype(jnp.int32)


def block_levels(own_key, shape, shards, smallest, largest):
    def one(axis_at, parts):
        draws = jax.random.uniform(jax.random.fold_in(jax.random.fold_in(own_key, 6), axis_at), (parts,), jnp.float32, smallest / len(shards), largest / len(shards))
        return jnp.repeat(jnp.exp(draws), shape[axis_at] // parts).reshape((-1,) + (1,) * (len(shape) - axis_at - 1))

    factor_of = one(*shards[0])
    for cut in shards[1:]:
        factor_of = factor_of * one(*cut)
    return factor_of


def scatter_about(stream_key, dims, deviation, reach, cuts=(), held_as=jnp.bfloat16):
    array = jax.random.normal(stream_key, dims, jnp.float32) * deviation
    if len(cuts) > 0:
        array = block_levels(stream_key, dims, cuts, -0.22, 0.18) * array
    return jnp.clip(array, min=-reach, max=reach).astype(held_as)


def setup_inputs(seed: int = 0) -> dict:
    key_of = jax.random.split(jax.random.key(seed), 4)
    return {
        "orbitals": scatter_about(key_of[0], (NORB, GX, GYZ), 1.0, 6.0, ((0, 64), (1, 4)), jnp.float32),
        "pair_table": draw_pair_table(jax.random.fold_in(key_of[3], 71), 0),
        "partner_offset": jax.random.randint(key_of[2], (1,), 1, N_BAND).astype(jnp.int32),
    }


SCREEN = 0.0025

def squares(length_all):
    modes = jnp.arange(length_all, dtype=jnp.float32)
    return 4.0 * jnp.sin(math.pi * modes / length_all) ** 2

def kernel_table():
    denominator = squares(GX)[:, None, None] + squares(GY)[None, :, None] + squares(GZ)[None, None, :]
    return 1.0 / (denominator + SCREEN)

def reference(orbitals, pair_table, partner_offset):
    rounded = lax.optimization_barrier(orbitals.astype(jnp.bfloat16))
    blocks = rounded.reshape(N_BAND, BLK, GX, GY, GZ)
    partner = partner_offset[0]
    first_band = pair_table[:, 0]
    second_band = pair_table[:, 1]
    kernel_full = kernel_table()

    def solve_block(block_index):
        own_rows = lax.dynamic_index_in_dim(blocks, block_index, 0, keepdims=False).astype(jnp.float32)
        visit_index = ((block_index - partner) % N_BAND).astype(jnp.int32)
        visit_rows = lax.dynamic_index_in_dim(blocks, visit_index, 0, keepdims=False).astype(jnp.float32)
        left_rows = own_rows[first_band]
        right_rows = visit_rows[second_band]
        densities = left_rows * right_rows
        spectrum = jnp.fft.fftn(densities, axes=(1, 2, 3))
        potential = jnp.real(jnp.fft.ifftn(spectrum * kernel_full, axes=(1, 2, 3)))
        zeros_block = jnp.zeros((BLK, GX, GY, GZ), dtype=jnp.float32)
        own_part = zeros_block.at[first_band].add(potential * right_rows)
        visit_part = zeros_block.at[second_band].add(potential * left_rows)
        return (own_part, visit_part)
    own_parts, visit_parts = lax.map(solve_block, jnp.arange(N_BAND, dtype=jnp.int32))
    field = own_parts + jnp.roll(visit_parts, -partner, axis=0)
    field = field.reshape(N_BAND, BLK, GX * GY * GZ)
    flat_orbitals = orbitals.reshape(N_BAND, BLK, GX * GY * GZ)
    gram = jnp.einsum('nac,nbc->nab', flat_orbitals, field, precision=lax.Precision.HIGHEST)
    gram = gram / math.sqrt(GX * GY * GZ)
    return (field.reshape(NORB, GX, GY * GZ), gram.reshape(NORB, BLK))
```

```python
import functools
import math

import jax
import jax.numpy as jnp
import ml_dtypes
import numpy as np
from jax import lax
from jax.experimental import pallas as pl
from jax.experimental.pallas import tpu as pltpu
from jax.sharding import PartitionSpec as P

N = 64
BLK = 8
PAIR = 4
SLAB = 16
LANES = 4096
SCREEN = 0.0025
TILES = 8
CHUNK = TILES * 128
XSTEP = 4
VMEM_LIMIT = 48 * 1024 * 1024

VMEM = pl.BlockSpec(memory_space=pltpu.VMEM)
SMEM = pl.BlockSpec(memory_space=pltpu.SMEM)


def cas_matrix():
    products = np.outer(np.arange(N), np.arange(N)) % N
    angles = 2.0 * math.pi / N * products
    return np.cos(angles) + np.sin(angles)


def halves(matrix):
    high = matrix.astype(ml_dtypes.bfloat16)
    low = (matrix - high.astype(np.float64)).astype(ml_dtypes.bfloat16)
    return high, low


def three(matrix):
    high, low = halves(matrix)
    return np.concatenate([high, high, low], axis=-1)


def tables():
    cas = cas_matrix()
    order = np.array(
        [[(q ^ d) * SLAB + r for d in range(PAIR) for r in range(SLAB)] for q in range(PAIR)]
    )
    x_forward = np.stack([three(cas[:, order[q]]) for q in range(PAIR)])
    x_back = np.stack([three(cas[order[q], :]) for q in range(PAIR)])
    y_both = three(cas)
    weave = np.zeros((2, 2, N, 2, 2, N))
    for source in range(2):
        for parity in range(2):
            weave[source, parity, :, parity, source, :] = cas
    weave = weave.reshape(4 * N, 4 * N)
    z_forward = np.stack(halves(weave))
    z_back = np.stack(halves(weave.T.copy()))
    squares = 4.0 * np.sin(math.pi * np.arange(N) / N) ** 2
    total = squares[:, None, None] + squares[None, :, None] + squares[None, None, :]
    kernel = 1.0 / (total + SCREEN) / N**3
    kernel = np.concatenate([kernel, kernel], axis=-1).astype(np.float32)
    return x_forward, x_back, y_both, z_forward, z_back, kernel


def pack(q_ref, table_ref, orb_ref, *refs):
    outs, (give_ref, take_ref) = refs[:-2], refs[-2:]
    own, minus, plus = outs[0:4], outs[4:8], outs[8:12]
    for p in range(BLK):
        first = table_ref[p, 0]
        second = table_ref[p, 1]
        give_ref[first] = second
        take_ref[second] = first
    for d in range(PAIR):
        base = (q_ref[0] ^ d) * 2
        for i in range(2):
            own[d][i] = orb_ref[base + i].astype(jnp.bfloat16)
            minus[d][i] = orb_ref[give_ref[base + i]].astype(jnp.bfloat16)
            plus[d][i] = orb_ref[take_ref[base + i]].astype(jnp.bfloat16)


def split(value):
    high = value.astype(jnp.bfloat16)
    low = (value - high.astype(jnp.float32)).astype(jnp.bfloat16)
    return high, low


def left_dot(table, value):
    high, low = split(value)
    stacked = jnp.concatenate([high, low, high], axis=0)
    return jnp.dot(table, stacked, preferred_element_type=jnp.float32)


def right_dot(value, table_ref):
    high, low = split(value)
    out = jnp.dot(high, table_ref[0], preferred_element_type=jnp.float32)
    out += jnp.dot(low, table_ref[0], preferred_element_type=jnp.float32)
    out += jnp.dot(high, table_ref[1], preferred_element_type=jnp.float32)
    return out


def solve(q_ref, *refs):
    own, minus, plus = refs[0:4], refs[4:8], refs[8:12]
    xf_ref, xb_ref, y_ref, zf_ref, zb_ref, k_ref = refs[12:18]
    outs, work = refs[18:22], refs[22]
    q = q_ref[0]
    cast = jnp.float32

    for a in range(2):

        @pl.loop(0, LANES // CHUNK)
        def _(c):
            at = pl.ds(pl.multiple_of(c * CHUNK, CHUNK), CHUNK)
            rows = [own[d][a, :, at].astype(cast) for d in range(PAIR)]
            dens_m = jnp.concatenate(
                [rows[d] * minus[d][a, :, at].astype(cast) for d in range(PAIR)], axis=0
            )
            dens_p = jnp.concatenate(
                [rows[d] * plus[d][a, :, at].astype(cast) for d in range(PAIR)], axis=0
            )
            both = jnp.concatenate(
                [s[:, t * 128 : t * 128 + 128] for t in range(TILES) for s in (dens_m, dens_p)],
                axis=1,
            )
            done_x = left_dot(xf_ref[q], both)
            tall = jnp.concatenate(
                [done_x[:, t * 256 : t * 256 + 256] for t in range(TILES)], axis=0
            )
            done_z = right_dot(tall, zf_ref)
            for t in range(TILES):
                part = done_z[t * N : t * N + N]
                y = (c * TILES + t) * 2
                work[a, pl.ds(pl.multiple_of(y * N, N), N), :] = part[:, :128]
                work[a, pl.ds(pl.multiple_of(y * N + N, N), N), :] = part[:, 128:]

    @pl.loop(0, N // XSTEP)
    def _(step):
        spots = [step * XSTEP + i for i in range(XSTEP)]
        value = jnp.concatenate(
            [work[a, pl.ds(x, N, stride=N), :] for x in spots for a in range(2)], axis=1
        )
        value = left_dot(y_ref[...], value)
        weight = jnp.concatenate([k_ref[x] for x in spots for a in range(2)], axis=1)
        value = left_dot(y_ref[...], value * weight)
        for i, x in enumerate(spots):
            for a in range(2):
                at = (i * 2 + a) * 128
                work[a, pl.ds(x, N, stride=N), :] = value[:, at : at + 128]

    for a in range(2):

        @pl.loop(0, LANES // CHUNK)
        def _(c):
            at = pl.ds(pl.multiple_of(c * CHUNK, CHUNK), CHUNK)
            parts = []
            for t in range(TILES):
                y = (c * TILES + t) * 2
                even = work[a, pl.ds(pl.multiple_of(y * N, N), N), :]
                odd = work[a, pl.ds(pl.multiple_of(y * N + N, N), N), :]
                parts.append(jnp.concatenate([even, odd], axis=1))
            done_z = right_dot(jnp.concatenate(parts, axis=0), zb_ref)
            wide = jnp.concatenate([done_z[t * N : t * N + N] for t in range(TILES)], axis=1)
            pot = left_dot(xb_ref[q], wide)
            pot_m = jnp.concatenate(
                [pot[:, t * 256 : t * 256 + 128] for t in range(TILES)], axis=1
            )
            pot_p = jnp.concatenate(
                [pot[:, t * 256 + 128 : t * 256 + 256] for t in range(TILES)], axis=1
            )
            for d in range(PAIR):
                here = slice(d * SLAB, d * SLAB + SLAB)
                field = pot_m[here] * minus[d][a, :, at].astype(cast)
                field += pot_p[here] * plus[d][a, :, at].astype(cast)
                outs[d][a, :, at] = field.astype(jnp.bfloat16)


def assemble(q_ref, orb_ref, *refs):
    parts, field_ref, gram_ref, flat = refs[0:4], refs[4], refs[5], refs[6]
    for d in range(PAIR):
        base = (q_ref[0] ^ d) * 2
        for i in range(2):
            rows = parts[d][i]
            field_ref[base + i] = rows.astype(jnp.float32)
            flat[pl.ds(pl.multiple_of((base + i) * SLAB, SLAB), SLAB), :] = rows
    rows = BLK * SLAB
    high, low = split(orb_ref[...].reshape(rows, LANES))
    dims = (((1,), (1,)), ((), ()))
    cross = lax.dot_general(high, flat[...], dims, preferred_element_type=jnp.float32)
    cross += lax.dot_general(low, flat[...], dims, preferred_element_type=jnp.float32)
    down = lax.broadcasted_iota(jnp.int32, (rows, rows), 0)
    along = lax.broadcasted_iota(jnp.int32, (rows, rows), 1)
    cross = jnp.where(down % SLAB == along % SLAB, cross, 0.0)
    summed = jnp.sum(cross.reshape(BLK, SLAB, rows), axis=1)
    pick_at = lax.broadcasted_iota(jnp.int32, (rows, BLK), 0) // SLAB
    pick = (pick_at == lax.broadcasted_iota(jnp.int32, (rows, BLK), 1)).astype(jnp.float32)
    gram_ref[...] = lax.dot_general(
        summed,
        pick,
        (((1,), (0,)), ((), ())),
        precision=lax.Precision.HIGHEST,
        preferred_element_type=jnp.float32,
    ) / math.sqrt(N**3)


PARAMS = pltpu.CompilerParams(vmem_limit_bytes=VMEM_LIMIT)
PIECE = jax.ShapeDtypeStruct((2, SLAB, LANES), jnp.bfloat16)


def on_device(bands, orbitals, pair_table, partner_offset):
    q = lax.axis_index("pair").astype(jnp.int32).reshape(1)
    packed = pl.pallas_call(
        pack,
        out_shape=[PIECE] * 12,
        in_specs=[SMEM, SMEM, VMEM],
        out_specs=[VMEM] * 12,
        scratch_shapes=[pltpu.SMEM((BLK,), jnp.int32)] * 2,
        compiler_params=PARAMS,
        name="pack",
    )(q, pair_table, orbitals)
    own, minus, plus = packed[0:4], packed[4:8], packed[8:12]

    def across(value, d):
        return lax.ppermute(value, "pair", [(i, i ^ d) for i in range(PAIR)])

    def moved(value, by, d):
        pairs = [
            (b * PAIR + i, (b + by) % bands * PAIR + (i ^ d))
            for b in range(bands)
            for i in range(PAIR)
        ]
        return lax.ppermute(value, ("band", "pair"), pairs)

    def shifted(by, operands):
        own, minus, plus = operands
        minus = [moved(minus[d], by, d) for d in range(PAIR)]
        plus = [moved(plus[d], -by, d) for d in range(PAIR)]
        own = [own[0]] + [across(own[d], d) for d in range(1, PAIR)]
        return own, minus, plus

    branches = [functools.partial(shifted, by) for by in range(1, bands)]
    own, minus, plus = lax.switch(partner_offset[0] - 1, branches, (own, minus, plus))
    consts = [jnp.asarray(t) for t in tables()]
    sent = pl.pallas_call(
        solve,
        out_shape=[PIECE] * 4,
        in_specs=[SMEM] + [VMEM] * 18,
        out_specs=[VMEM] * 4,
        scratch_shapes=[pltpu.VMEM((2, N * N, 128), jnp.float32)],
        compiler_params=PARAMS,
        name="solve",
    )(q, *own, *minus, *plus, *consts)
    back = [sent[0]] + [across(sent[d], d) for d in range(1, PAIR)]
    field, gram = pl.pallas_call(
        assemble,
        out_shape=[
            jax.ShapeDtypeStruct((BLK, SLAB, LANES), jnp.float32),
            jax.ShapeDtypeStruct((BLK, BLK), jnp.float32),
        ],
        in_specs=[SMEM] + [VMEM] * 5,
        out_specs=[VMEM] * 2,
        scratch_shapes=[pltpu.VMEM((BLK * SLAB, LANES), jnp.bfloat16)],
        compiler_params=PARAMS,
        name="assemble",
    )(q, orbitals, *back)
    return field, lax.psum(gram, "pair")


def solution(mesh):
    return jax.shard_map(
        functools.partial(on_device, mesh.shape["band"]),
        mesh=mesh,
        in_specs=(P("band", "pair", None), P(), P()),
        out_specs=(P("band", "pair", None), P("band", None)),
        check_vma=False,
    )
```

```python
import math

import jax
import jax.numpy as jnp
import ml_dtypes
import numpy as np
from jax import lax
from jax.experimental import pallas as pl
from jax.experimental.pallas import tpu as pltpu
from jax.sharding import PartitionSpec as P

N = 64
BLK = 8
PAIR = 4
SLAB = 16
LANES = 4096
SCREEN = 0.0025
TILES = 8
CHUNK = TILES * 128
XSTEP = 8
SUB = 8
SPOTS = 64
VMEM_LIMIT = 48 * 1024 * 1024

VMEM = pl.BlockSpec(memory_space=pltpu.VMEM)
SMEM = pl.BlockSpec(memory_space=pltpu.SMEM)


def cas_matrix():
    products = np.outer(np.arange(N), np.arange(N)) % N
    angles = 2.0 * math.pi / N * products
    return np.cos(angles) + np.sin(angles)


def halves(matrix):
    high = matrix.astype(ml_dtypes.bfloat16)
    low = (matrix - high.astype(np.float64)).astype(ml_dtypes.bfloat16)
    return high, low


def three(matrix):
    high, low = halves(matrix)
    return np.concatenate([high, high, low], axis=-1)


def tables():
    cas = cas_matrix()
    order = np.array(
        [
            [(q ^ d) * SLAB + h * SUB + r for h in range(2) for d in range(PAIR) for r in range(SUB)]
            for q in range(PAIR)
        ]
    )
    x_forward = np.stack([three(cas[:, order[q]]) for q in range(PAIR)])
    x_back = np.stack([three(cas[order[q], :]) for q in range(PAIR)])
    y_both = three(cas)
    weave = np.zeros((2, 2, N, 2, 2, N))
    for source in range(2):
        for parity in range(2):
            weave[source, parity, :, parity, source, :] = cas
    weave = weave.reshape(4 * N, 4 * N)
    z_forward = np.stack(halves(weave))
    z_back = np.stack(halves(weave.T.copy()))
    squares = 4.0 * np.sin(math.pi * np.arange(N) / N) ** 2
    total = squares[:, None, None] + squares[None, :, None] + squares[None, None, :]
    kernel = 1.0 / (total + SCREEN) / N**3
    kernel = np.concatenate([kernel, kernel], axis=-1).astype(np.float32)
    return x_forward, x_back, y_both, z_forward, z_back, kernel


def arrange(q_ref, orb_ref, spread_ref, *own):
    for t in range(LANES // 128):
        part = orb_ref[:, :, t * 128 : t * 128 + 128]
        for h in range(2):
            rows = part[:, h * SUB : h * SUB + SUB, :].reshape(BLK * SUB, 128)
            spread_ref[t * 2 + h] = rows.astype(jnp.bfloat16)
    for d in range(PAIR):
        base = (q_ref[0] ^ d) * 2
        for i in range(2):
            own[d][i] = orb_ref[base + i].astype(jnp.bfloat16)


def route(table_ref, offset_ref, held_ref, out_ref, wide, give_ref, take_ref):
    for p in range(BLK):
        first = table_ref[p, 0]
        second = table_ref[p, 1]
        give_ref[first] = second
        take_ref[second] = first

    @pl.loop(0, SPOTS, unroll=4)
    def _(j):
        wide[j] = held_ref[j].astype(jnp.float32).reshape(BLK, SUB, 128)

    @pl.loop(0, SPOTS)
    def _(b):
        below = lax.rem(b - offset_ref[0] + SPOTS, SPOTS)
        above = lax.rem(b + offset_ref[0], SPOTS)
        for q in range(PAIR):
            rows = []
            for i in range(2):
                rows.append(wide[below, give_ref[q * 2 + i]])
                rows.append(wide[above, take_ref[q * 2 + i]])
            out_ref[b * PAIR + q] = jnp.concatenate(rows, axis=0).astype(jnp.bfloat16)


def split(value):
    high = value.astype(jnp.bfloat16)
    low = (value - high.astype(jnp.float32)).astype(jnp.bfloat16)
    return high, low


def left_dot(table, value):
    high, low = split(value)
    stacked = jnp.concatenate([high, low, high], axis=0)
    return jnp.dot(table, stacked, preferred_element_type=jnp.float32)


def right_dot(value, table_ref):
    high, low = split(value)
    out = jnp.dot(high, table_ref[0], preferred_element_type=jnp.float32)
    out += jnp.dot(low, table_ref[0], preferred_element_type=jnp.float32)
    out += jnp.dot(high, table_ref[1], preferred_element_type=jnp.float32)
    return out


def solve(q_ref, *refs):
    own, seen = refs[0:4], refs[4]
    xf_ref, xb_ref, y_ref, zf_ref, zb_ref, k_ref = refs[5:11]
    outs, work = refs[11:15], refs[15]
    q = q_ref[0]
    cast = jnp.float32

    def visiting(tile):
        below, above = [], []
        for h in range(2):
            for d in range(PAIR):
                rows = seen[(tile * 2 + h) * PAIR + (q ^ d)].astype(cast)
                below.append(rows[:SUB])
                above.append(rows[SUB:])
        return jnp.concatenate(below, axis=0), jnp.concatenate(above, axis=0)

    @pl.loop(0, LANES // CHUNK)
    def _(c):
        wide = []
        for t in range(TILES):
            tile = c * TILES + t
            at = pl.ds(pl.multiple_of(tile * 128, 128), 128)
            slabs = [own[d][0, :, at].astype(cast) for d in range(PAIR)]
            mine = jnp.concatenate(
                [slabs[d][h * SUB : h * SUB + SUB] for h in range(2) for d in range(PAIR)], axis=0
            )
            below, above = visiting(tile)
            wide += [mine * below, mine * above]
        done_x = left_dot(xf_ref[q], jnp.concatenate(wide, axis=1))
        tall = jnp.concatenate(
            [done_x[:, t * 256 : t * 256 + 256] for t in range(TILES)], axis=0
        )
        done_z = right_dot(tall, zf_ref)
        for t in range(TILES):
            part = done_z[t * N : t * N + N]
            y = (c * TILES + t) * 2
            work[pl.ds(pl.multiple_of(y * N, N), N), :] = part[:, :128]
            work[pl.ds(pl.multiple_of(y * N + N, N), N), :] = part[:, 128:]

    @pl.loop(0, N // XSTEP)
    def _(step):
        spots = [step * XSTEP + i for i in range(XSTEP)]
        value = jnp.concatenate([work[pl.ds(x, N, stride=N), :] for x in spots], axis=1)
        value = left_dot(y_ref[...], value)
        weight = jnp.concatenate([k_ref[x] for x in spots], axis=1)
        value = left_dot(y_ref[...], value * weight)
        for i, x in enumerate(spots):
            work[pl.ds(x, N, stride=N), :] = value[:, i * 128 : i * 128 + 128]

    @pl.loop(0, LANES // CHUNK)
    def _(c):
        parts = []
        for t in range(TILES):
            y = (c * TILES + t) * 2
            even = work[pl.ds(pl.multiple_of(y * N, N), N), :]
            odd = work[pl.ds(pl.multiple_of(y * N + N, N), N), :]
            parts.append(jnp.concatenate([even, odd], axis=1))
        done_z = right_dot(jnp.concatenate(parts, axis=0), zb_ref)
        wide = jnp.concatenate([done_z[t * N : t * N + N] for t in range(TILES)], axis=1)
        pot = left_dot(xb_ref[q], wide)
        for t in range(TILES):
            tile = c * TILES + t
            at = pl.ds(pl.multiple_of(tile * 128, 128), 128)
            below, above = visiting(tile)
            field = pot[:, t * 256 : t * 256 + 128] * below
            field += pot[:, t * 256 + 128 : t * 256 + 256] * above
            for d in range(PAIR):
                rows = [
                    field[(h * PAIR + d) * SUB : (h * PAIR + d + 1) * SUB] for h in range(2)
                ]
                outs[d][:, at] = jnp.concatenate(rows, axis=0).astype(jnp.bfloat16)


def assemble(q_ref, orb_ref, *refs):
    parts, field_ref, gram_ref, flat = refs[0:8], refs[8], refs[9], refs[10]
    for d in range(PAIR):
        base = (q_ref[0] ^ d) * 2
        for i in range(2):
            rows = parts[i * PAIR + d][...]
            field_ref[base + i] = rows.astype(jnp.float32)
            flat[pl.ds(pl.multiple_of((base + i) * SLAB, SLAB), SLAB), :] = rows
    rows = BLK * SLAB
    high, low = split(orb_ref[...].reshape(rows, LANES))
    dims = (((1,), (1,)), ((), ()))
    cross = lax.dot_general(high, flat[...], dims, preferred_element_type=jnp.float32)
    cross += lax.dot_general(low, flat[...], dims, preferred_element_type=jnp.float32)
    down = lax.broadcasted_iota(jnp.int32, (rows, rows), 0)
    along = lax.broadcasted_iota(jnp.int32, (rows, rows), 1)
    cross = jnp.where(down % SLAB == along % SLAB, cross, 0.0)
    summed = jnp.sum(cross.reshape(BLK, SLAB, rows), axis=1)
    pick_at = lax.broadcasted_iota(jnp.int32, (rows, BLK), 0) // SLAB
    pick = (pick_at == lax.broadcasted_iota(jnp.int32, (rows, BLK), 1)).astype(jnp.float32)
    gram_ref[...] = lax.dot_general(
        summed,
        pick,
        (((1,), (0,)), ((), ())),
        precision=lax.Precision.HIGHEST,
        preferred_element_type=jnp.float32,
    ) / math.sqrt(N**3)


PARAMS = pltpu.CompilerParams(vmem_limit_bytes=VMEM_LIMIT)
PIECE = jax.ShapeDtypeStruct((2, SLAB, LANES), jnp.bfloat16)
SENT = jax.ShapeDtypeStruct((SLAB, LANES), jnp.bfloat16)


def on_device(orbitals, pair_table, partner_offset):
    q = lax.axis_index("pair").astype(jnp.int32).reshape(1)

    def across(value, d):
        return lax.ppermute(value, "pair", [(i, i ^ d) for i in range(PAIR)])

    spread, *own = pl.pallas_call(
        arrange,
        out_shape=[jax.ShapeDtypeStruct((SPOTS, BLK * SUB, 128), jnp.bfloat16)] + [PIECE] * 4,
        in_specs=[SMEM, VMEM],
        out_specs=[VMEM] * 5,
        compiler_params=PARAMS,
        name="arrange",
    )(q, orbitals)
    own = [own[0]] + [across(own[d], d) for d in range(1, PAIR)]
    held = lax.all_to_all(spread, "band", 0, 0, tiled=True)
    routed = pl.pallas_call(
        route,
        out_shape=jax.ShapeDtypeStruct((SPOTS * PAIR, 4 * SUB, 128), jnp.bfloat16),
        in_specs=[SMEM, SMEM, VMEM],
        out_specs=VMEM,
        scratch_shapes=[
            pltpu.VMEM((SPOTS, BLK, SUB, 128), jnp.float32),
            pltpu.SMEM((BLK,), jnp.int32),
            pltpu.SMEM((BLK,), jnp.int32),
        ],
        compiler_params=PARAMS,
        name="route",
    )(pair_table, partner_offset, held)
    seen = lax.all_to_all(routed, ("band", "pair"), 0, 0, tiled=True)
    consts = [jnp.asarray(t) for t in tables()]
    back = []
    for a in range(2):
        one = pl.BlockSpec((1, SLAB, LANES), lambda i, a=a: (a, 0, 0))
        rows = pl.BlockSpec((SPOTS * PAIR, 2 * SUB, 128), lambda i, a=a: (0, a, 0))
        sent = pl.pallas_call(
            solve,
            grid=(1,),
            out_shape=[SENT] * 4,
            in_specs=[SMEM] + [one] * 4 + [rows] + [VMEM] * 6,
            out_specs=[VMEM] * 4,
            scratch_shapes=[pltpu.VMEM((N * N, 128), jnp.float32)],
            compiler_params=PARAMS,
            cost_estimate=pl.CostEstimate(
                flops=10_000_000_000, bytes_accessed=8_000_000, transcendentals=0
            ),
            name="solve",
        )(q, *own, seen, *consts)
        back += [sent[0]] + [across(sent[d], d) for d in range(1, PAIR)]
    field, gram = pl.pallas_call(
        assemble,
        out_shape=[
            jax.ShapeDtypeStruct((BLK, SLAB, LANES), jnp.float32),
            jax.ShapeDtypeStruct((BLK, BLK), jnp.float32),
        ],
        in_specs=[SMEM] + [VMEM] * 9,
        out_specs=[VMEM] * 2,
        scratch_shapes=[pltpu.VMEM((BLK * SLAB, LANES), jnp.bfloat16)],
        compiler_params=PARAMS,
        name="assemble",
    )(q, orbitals, *back)
    return field, (gram + across(gram, 1)) + (across(gram, 2) + across(gram, 3))


def solution(mesh):
    return jax.shard_map(
        on_device,
        mesh=mesh,
        in_specs=(P("band", "pair", None), P(), P()),
        out_specs=(P("band", "pair", None), P("band", None)),
        check_vma=False,
    )
```

```python
import math

import jax
import jax.numpy as jnp
import ml_dtypes
import numpy as np
from jax import lax
from jax.experimental import pallas as pl
from jax.experimental.pallas import tpu as pltpu
from jax.sharding import PartitionSpec as P

N = 64
BLK = 8
PAIR = 4
SLAB = 16
LANES = 4096
SCREEN = 0.0025
TILES = 32
CHUNK = TILES * 128
XSTEP = 32
PITCH = 72
SUB = 8
SPOTS = 64
VMEM_LIMIT = 48 * 1024 * 1024

VMEM = pl.BlockSpec(memory_space=pltpu.VMEM)
SMEM = pl.BlockSpec(memory_space=pltpu.SMEM)


def cas_matrix():
    products = np.outer(np.arange(N), np.arange(N)) % N
    angles = 2.0 * math.pi / N * products
    return np.cos(angles) + np.sin(angles)


def halves(matrix):
    high = matrix.astype(ml_dtypes.bfloat16)
    low = (matrix - high.astype(np.float64)).astype(ml_dtypes.bfloat16)
    return high, low


def three(matrix):
    high, low = halves(matrix)
    return np.concatenate([high, high, low], axis=-1)


def tables():
    cas = cas_matrix()
    order = np.array(
        [
            [(q ^ d) * SLAB + h * SUB + r for h in range(2) for d in range(PAIR) for r in range(SUB)]
            for q in range(PAIR)
        ]
    )
    x_forward = np.stack([three(cas[:, order[q]]) for q in range(PAIR)])
    x_back = np.stack([three(cas[order[q], :]) for q in range(PAIR)])
    y_both = three(cas)
    weave = np.zeros((2, 2, N, 2, 2, N))
    for source in range(2):
        for parity in range(2):
            weave[source, parity, :, parity, source, :] = cas
    weave = weave.reshape(4 * N, 4 * N)
    z_forward = np.stack(halves(weave))
    z_back = np.stack(halves(weave.T.copy()))
    squares = 4.0 * np.sin(math.pi * np.arange(N) / N) ** 2
    total = squares[:, None, None] + squares[None, :, None] + squares[None, None, :]
    kernel = 1.0 / (total + SCREEN) / N**3
    kernel = np.concatenate([kernel, kernel], axis=-1).astype(np.float32)
    return x_forward, x_back, y_both, z_forward, z_back, kernel


def arrange(q_ref, orb_ref, spread_ref, *own):
    for t in range(LANES // 128):
        part = orb_ref[:, :, t * 128 : t * 128 + 128]
        for h in range(2):
            rows = part[:, h * SUB : h * SUB + SUB, :].reshape(BLK * SUB, 128)
            spread_ref[t * 2 + h] = rows.astype(jnp.bfloat16)
    for d in range(PAIR):
        base = (q_ref[0] ^ d) * 2
        for i in range(2):
            own[d][i] = orb_ref[base + i].astype(jnp.bfloat16)


def route(table_ref, offset_ref, held_ref, out_ref, wide, give_ref, take_ref):
    for p in range(BLK):
        first = table_ref[p, 0]
        second = table_ref[p, 1]
        give_ref[first] = second
        take_ref[second] = first

    @pl.loop(0, SPOTS, unroll=4)
    def _(j):
        wide[j] = held_ref[j].astype(jnp.float32).reshape(BLK, SUB, 128)

    @pl.loop(0, SPOTS)
    def _(b):
        below = lax.rem(b - offset_ref[0] + SPOTS, SPOTS)
        above = lax.rem(b + offset_ref[0], SPOTS)
        for q in range(PAIR):
            rows = []
            for i in range(2):
                rows.append(wide[below, give_ref[q * 2 + i]])
                rows.append(wide[above, take_ref[q * 2 + i]])
            out_ref[b * PAIR + q] = jnp.concatenate(rows, axis=0).astype(jnp.bfloat16)


def split(value):
    high = value.astype(jnp.bfloat16)
    low = (value - high.astype(jnp.float32)).astype(jnp.bfloat16)
    return high, low


def left_dot(table, value):
    high, low = split(value)
    stacked = jnp.concatenate([high, low, high], axis=0)
    return jnp.dot(table, stacked, preferred_element_type=jnp.float32)


def right_dot(value, table_ref):
    high, low = split(value)
    out = jnp.dot(high, table_ref[0], preferred_element_type=jnp.float32)
    out += jnp.dot(low, table_ref[0], preferred_element_type=jnp.float32)
    out += jnp.dot(high, table_ref[1], preferred_element_type=jnp.float32)
    return out


def solve(q_ref, *refs):
    own, seen = refs[0:4], refs[4]
    xf_ref, xb_ref, y_ref, zf_ref, zb_ref, k_ref = refs[5:11]
    outs, work = refs[11:15], refs[15]
    q = q_ref[0]
    cast = jnp.float32

    def visiting(tile):
        below, above = [], []
        for h in range(2):
            for d in range(PAIR):
                rows = seen[(tile * 2 + h) * PAIR + (q ^ d)].astype(cast)
                below.append(rows[:SUB])
                above.append(rows[SUB:])
        return jnp.concatenate(below, axis=0), jnp.concatenate(above, axis=0)

    @pl.loop(0, LANES // CHUNK)
    def _(c):
        wide = []
        for t in range(TILES):
            tile = c * TILES + t
            at = pl.ds(pl.multiple_of(tile * 128, 128), 128)
            slabs = [own[d][0, :, at].astype(cast) for d in range(PAIR)]
            mine = jnp.concatenate(
                [slabs[d][h * SUB : h * SUB + SUB] for h in range(2) for d in range(PAIR)], axis=0
            )
            below, above = visiting(tile)
            wide += [mine * below, mine * above]
        done_x = left_dot(xf_ref[q], jnp.concatenate(wide, axis=1))
        tall = jnp.concatenate(
            [done_x[:, t * 256 : t * 256 + 256] for t in range(TILES)], axis=0
        )
        done_z = right_dot(tall, zf_ref)
        for t in range(TILES):
            part = done_z[t * N : t * N + N]
            y = (c * TILES + t) * 2
            work[pl.ds(pl.multiple_of(y * PITCH, 8), N), :] = part[:, :128]
            work[pl.ds(pl.multiple_of(y * PITCH + PITCH, 8), N), :] = part[:, 128:]

    @pl.loop(0, N // XSTEP)
    def _(step):
        spots = [step * XSTEP + i for i in range(XSTEP)]
        value = jnp.concatenate([work[pl.ds(x, N, stride=PITCH), :] for x in spots], axis=1)
        value = left_dot(y_ref[...], value)
        weight = jnp.concatenate([k_ref[x] for x in spots], axis=1)
        value = left_dot(y_ref[...], value * weight)
        for i, x in enumerate(spots):
            work[pl.ds(x, N, stride=PITCH), :] = value[:, i * 128 : i * 128 + 128]

    @pl.loop(0, LANES // CHUNK)
    def _(c):
        parts = []
        for t in range(TILES):
            y = (c * TILES + t) * 2
            even = work[pl.ds(pl.multiple_of(y * PITCH, 8), N), :]
            odd = work[pl.ds(pl.multiple_of(y * PITCH + PITCH, 8), N), :]
            parts.append(jnp.concatenate([even, odd], axis=1))
        done_z = right_dot(jnp.concatenate(parts, axis=0), zb_ref)
        wide = jnp.concatenate([done_z[t * N : t * N + N] for t in range(TILES)], axis=1)
        pot = left_dot(xb_ref[q], wide)
        for t in range(TILES):
            tile = c * TILES + t
            at = pl.ds(pl.multiple_of(tile * 128, 128), 128)
            below, above = visiting(tile)
            field = pot[:, t * 256 : t * 256 + 128] * below
            field += pot[:, t * 256 + 128 : t * 256 + 256] * above
            for d in range(PAIR):
                rows = [
                    field[(h * PAIR + d) * SUB : (h * PAIR + d + 1) * SUB] for h in range(2)
                ]
                outs[d][:, at] = jnp.concatenate(rows, axis=0).astype(jnp.bfloat16)


def assemble(q_ref, orb_ref, *refs):
    parts, field_ref, gram_ref, flat = refs[0:8], refs[8], refs[9], refs[10]
    for d in range(PAIR):
        base = (q_ref[0] ^ d) * 2
        for i in range(2):
            rows = parts[i * PAIR + d][...]
            field_ref[base + i] = rows.astype(jnp.float32)
            flat[pl.ds(pl.multiple_of((base + i) * SLAB, SLAB), SLAB), :] = rows
    rows = BLK * SLAB
    high, low = split(orb_ref[...].reshape(rows, LANES))
    dims = (((1,), (1,)), ((), ()))
    cross = lax.dot_general(high, flat[...], dims, preferred_element_type=jnp.float32)
    cross += lax.dot_general(low, flat[...], dims, preferred_element_type=jnp.float32)
    down = lax.broadcasted_iota(jnp.int32, (rows, rows), 0)
    along = lax.broadcasted_iota(jnp.int32, (rows, rows), 1)
    cross = jnp.where(down % SLAB == along % SLAB, cross, 0.0)
    summed = jnp.sum(cross.reshape(BLK, SLAB, rows), axis=1)
    pick_at = lax.broadcasted_iota(jnp.int32, (rows, BLK), 0) // SLAB
    pick = (pick_at == lax.broadcasted_iota(jnp.int32, (rows, BLK), 1)).astype(jnp.float32)
    gram_ref[...] = lax.dot_general(
        summed,
        pick,
        (((1,), (0,)), ((), ())),
        precision=lax.Precision.HIGHEST,
        preferred_element_type=jnp.float32,
    ) / math.sqrt(N**3)


PARAMS = pltpu.CompilerParams(vmem_limit_bytes=VMEM_LIMIT)
PIECE = jax.ShapeDtypeStruct((2, SLAB, LANES), jnp.bfloat16)
SENT = jax.ShapeDtypeStruct((SLAB, LANES), jnp.bfloat16)


def on_device(orbitals, pair_table, partner_offset):
    q = lax.axis_index("pair").astype(jnp.int32).reshape(1)

    def across(value, d):
        return lax.ppermute(value, "pair", [(i, i ^ d) for i in range(PAIR)])

    spread, *own = pl.pallas_call(
        arrange,
        out_shape=[jax.ShapeDtypeStruct((SPOTS, BLK * SUB, 128), jnp.bfloat16)] + [PIECE] * 4,
        in_specs=[SMEM, VMEM],
        out_specs=[VMEM] * 5,
        compiler_params=PARAMS,
        name="arrange",
    )(q, orbitals)
    own = [own[0]] + [across(own[d], d) for d in range(1, PAIR)]
    held = lax.all_to_all(spread, "band", 0, 0, tiled=True)
    routed = pl.pallas_call(
        route,
        out_shape=jax.ShapeDtypeStruct((SPOTS * PAIR, 4 * SUB, 128), jnp.bfloat16),
        in_specs=[SMEM, SMEM, VMEM],
        out_specs=VMEM,
        scratch_shapes=[
            pltpu.VMEM((SPOTS, BLK, SUB, 128), jnp.float32),
            pltpu.SMEM((BLK,), jnp.int32),
            pltpu.SMEM((BLK,), jnp.int32),
        ],
        compiler_params=PARAMS,
        name="route",
    )(pair_table, partner_offset, held)
    seen = lax.all_to_all(routed, ("band", "pair"), 0, 0, tiled=True)
    consts = [jnp.asarray(t) for t in tables()]
    back = []
    for a in range(2):
        one = pl.BlockSpec((1, SLAB, LANES), lambda i, a=a: (a, 0, 0))
        rows = pl.BlockSpec((SPOTS * PAIR, 2 * SUB, 128), lambda i, a=a: (0, a, 0))
        sent = pl.pallas_call(
            solve,
            grid=(1,),
            out_shape=[SENT] * 4,
            in_specs=[SMEM] + [one] * 4 + [rows] + [VMEM] * 6,
            out_specs=[VMEM] * 4,
            scratch_shapes=[pltpu.VMEM((N * PITCH, 128), jnp.float32)],
            compiler_params=PARAMS,
            cost_estimate=pl.CostEstimate(
                flops=10_000_000_000, bytes_accessed=8_000_000, transcendentals=0
            ),
            name="solve",
        )(q, *own, seen, *consts)
        back += [sent[0]] + [across(sent[d], d) for d in range(1, PAIR)]
    field, gram = pl.pallas_call(
        assemble,
        out_shape=[
            jax.ShapeDtypeStruct((BLK, SLAB, LANES), jnp.float32),
            jax.ShapeDtypeStruct((BLK, BLK), jnp.float32),
        ],
        in_specs=[SMEM] + [VMEM] * 9,
        out_specs=[VMEM] * 2,
        scratch_shapes=[pltpu.VMEM((BLK * SLAB, LANES), jnp.bfloat16)],
        compiler_params=PARAMS,
        name="assemble",
    )(q, orbitals, *back)
    return field, (gram + across(gram, 1)) + (across(gram, 2) + across(gram, 3))


def solution(mesh):
    return jax.shard_map(
        on_device,
        mesh=mesh,
        in_specs=(P("band", "pair", None), P(), P()),
        out_specs=(P("band", "pair", None), P("band", None)),
        check_vma=False,
    )
```

```python
import functools
import math

import jax
import jax.numpy as jnp
import ml_dtypes
import numpy as np
from jax import lax
from jax.experimental import pallas as pl
from jax.experimental.pallas import tpu as pltpu
from jax.sharding import PartitionSpec as P

N = 64
BLK = 8
PAIR = 4
SLAB = 16
LANES = 4096
SCREEN = 0.0025
TILES = 32
CHUNK = TILES * 128
XSTEP = 32
PITCH = 72
SUB = 8
SPOTS = 64
STEPS = 4
X_FORWARD = 0
X_BACK = 256
Z_FORWARD = 512
Z_BACK = 1024
Y_BOTH = 1536
ROWS = 4096
VMEM_LIMIT = 48 * 1024 * 1024

VMEM = pl.BlockSpec(memory_space=pltpu.VMEM)
SMEM = pl.BlockSpec(memory_space=pltpu.SMEM)
HBM = pl.BlockSpec(memory_space=pltpu.HBM)


def cas_matrix():
    products = np.outer(np.arange(N), np.arange(N)) % N
    angles = 2.0 * math.pi / N * products
    return np.cos(angles) + np.sin(angles)


def halves(matrix):
    high = matrix.astype(ml_dtypes.bfloat16)
    low = (matrix - high.astype(np.float64)).astype(ml_dtypes.bfloat16)
    return high, low


def three(matrix):
    high, low = halves(matrix)
    return np.concatenate([high, high, low], axis=-1)


def tables():
    cas = cas_matrix()
    order = np.array(
        [
            [(q ^ d) * SLAB + h * SUB + r for h in range(2) for d in range(PAIR) for r in range(SUB)]
            for q in range(PAIR)
        ]
    )
    x_forward = np.stack([three(cas[:, order[q]]) for q in range(PAIR)])
    x_back = np.stack([three(cas[order[q], :]) for q in range(PAIR)])
    y_both = three(cas)
    weave = np.zeros((2, 2, N, 2, 2, N))
    for source in range(2):
        for parity in range(2):
            weave[source, parity, :, parity, source, :] = cas
    weave = weave.reshape(4 * N, 4 * N)
    z_forward = np.stack(halves(weave))
    z_back = np.stack(halves(weave.T.copy()))
    squares = 4.0 * np.sin(math.pi * np.arange(N) / N) ** 2
    total = squares[:, None, None] + squares[None, :, None] + squares[None, None, :]
    kernel = 1.0 / (total + SCREEN) / N**3
    kernel = np.concatenate([kernel, kernel], axis=-1).astype(np.float32)
    packed = np.zeros((ROWS, 4 * N), ml_dtypes.bfloat16)
    packed[X_FORWARD : X_FORWARD + PAIR * N, : 3 * N] = x_forward.reshape(PAIR * N, 3 * N)
    packed[X_BACK : X_BACK + PAIR * N, : 3 * N] = x_back.reshape(PAIR * N, 3 * N)
    packed[Z_FORWARD : Z_FORWARD + 8 * N] = z_forward.reshape(8 * N, 4 * N)
    packed[Z_BACK : Z_BACK + 8 * N] = z_back.reshape(8 * N, 4 * N)
    packed[Y_BOTH : Y_BOTH + N, : 3 * N] = y_both
    return packed, kernel


def arrange(q_ref, orb_ref, spread_ref, *own):
    for t in range(LANES // 128):
        part = orb_ref[:, :, t * 128 : t * 128 + 128]
        for h in range(2):
            rows = part[:, h * SUB : h * SUB + SUB, :].reshape(BLK * SUB, 128)
            spread_ref[t * 2 + h] = rows.astype(jnp.bfloat16)
    for d in range(PAIR):
        base = (q_ref[0] ^ d) * 2
        for i in range(2):
            own[d][i] = orb_ref[base + i].astype(jnp.bfloat16)


def route(table_ref, offset_ref, held_ref, out_ref, wide, give_ref, take_ref):
    for p in range(BLK):
        first = table_ref[p, 0]
        second = table_ref[p, 1]
        give_ref[first] = second
        take_ref[second] = first

    gives = [give_ref[band] * SUB for band in range(BLK)]
    takes = [take_ref[band] * SUB for band in range(BLK)]
    offset = offset_ref[0]

    def picked(start):
        return wide[pl.ds(pl.multiple_of(start, SUB), SUB), :]

    @pl.when(pl.program_id(0) == 0)
    def _():
        @pl.loop(0, SPOTS, unroll=4)
        def _(j):
            at = pl.ds(pl.multiple_of(j * BLK * SUB, BLK * SUB), BLK * SUB)
            wide[at, :] = held_ref[j].astype(jnp.float32)

    @pl.loop(0, SPOTS // STEPS, unroll=4)
    def _(at):
        b = pl.program_id(0) * (SPOTS // STEPS) + at
        below = ((b - offset) & (SPOTS - 1)) * (BLK * SUB)
        above = ((b + offset) & (SPOTS - 1)) * (BLK * SUB)
        for q in range(PAIR):
            rows = []
            for band in (q * 2, q * 2 + 1):
                rows += [picked(below + gives[band]), picked(above + takes[band])]
            out_ref[at * PAIR + q] = jnp.concatenate(rows, axis=0).astype(jnp.bfloat16)


def split(value):
    high = value.astype(jnp.bfloat16)
    low = (value - high.astype(jnp.float32)).astype(jnp.bfloat16)
    return high, low


def left_dot(table, value):
    high, low = split(value)
    stacked = jnp.concatenate([high, low, high], axis=0)
    return jnp.dot(table, stacked, preferred_element_type=jnp.float32)


def right_dot(value, table_ref):
    high, low = split(value)
    out = jnp.dot(high, table_ref[: 4 * N], preferred_element_type=jnp.float32)
    out += jnp.dot(low, table_ref[: 4 * N], preferred_element_type=jnp.float32)
    out += jnp.dot(high, table_ref[4 * N :], preferred_element_type=jnp.float32)
    return out


def solve(a, q_ref, *refs):
    own, seen = refs[0:4], refs[4]
    packed, kernel, outs, work = refs[5], refs[6], refs[7:11], refs[11]
    xf_ref, zf_ref, y_ref, k_ref, zb_ref, xb_ref = rooms = refs[12:18]
    sems = refs[18]
    q = q_ref[0]
    cast = jnp.float32
    here = pl.multiple_of(q * N, N)
    sources = (
        packed.at[pl.ds(X_FORWARD + here, N)],
        packed.at[pl.ds(Z_FORWARD, 8 * N)],
        packed.at[pl.ds(Y_BOTH, N)],
        kernel,
        packed.at[pl.ds(Z_BACK, 8 * N)],
        packed.at[pl.ds(X_BACK + here, N)],
    )
    loads = [
        pltpu.make_async_copy(source, room, sems.at[n])
        for n, (source, room) in enumerate(zip(sources, rooms))
    ]
    for load in loads:
        load.start()
    rows_at = slice(a * 2 * SUB, (a + 1) * 2 * SUB)

    def visiting(tile):
        below, above = [], []
        for h in range(2):
            for d in range(PAIR):
                rows = seen[(tile * 2 + h) * PAIR + (q ^ d), rows_at].astype(cast)
                below.append(rows[:SUB])
                above.append(rows[SUB:])
        return jnp.concatenate(below, axis=0), jnp.concatenate(above, axis=0)

    loads[0].wait()
    loads[1].wait()

    @pl.loop(0, LANES // CHUNK)
    def _(c):
        wide = []
        for t in range(TILES):
            tile = c * TILES + t
            at = pl.ds(pl.multiple_of(tile * 128, 128), 128)
            slabs = [own[d][a, :, at].astype(cast) for d in range(PAIR)]
            mine = jnp.concatenate(
                [slabs[d][h * SUB : h * SUB + SUB] for h in range(2) for d in range(PAIR)], axis=0
            )
            below, above = visiting(tile)
            wide += [mine * below, mine * above]
        done_x = left_dot(xf_ref[:, : 3 * N], jnp.concatenate(wide, axis=1))
        tall = jnp.concatenate(
            [done_x[:, t * 256 : t * 256 + 256] for t in range(TILES)], axis=0
        )
        done_z = right_dot(tall, zf_ref)
        for t in range(TILES):
            part = done_z[t * N : t * N + N]
            y = (c * TILES + t) * 2
            work[pl.ds(pl.multiple_of(y * PITCH, 8), N), :] = part[:, :128]
            work[pl.ds(pl.multiple_of(y * PITCH + PITCH, 8), N), :] = part[:, 128:]

    loads[2].wait()
    loads[3].wait()

    @pl.loop(0, N // XSTEP)
    def _(step):
        spots = [step * XSTEP + i for i in range(XSTEP)]
        value = jnp.concatenate([work[pl.ds(x, N, stride=PITCH), :] for x in spots], axis=1)
        value = left_dot(y_ref[:, : 3 * N], value)
        weight = jnp.concatenate([k_ref[x] for x in spots], axis=1)
        value = left_dot(y_ref[:, : 3 * N], value * weight)
        for i, x in enumerate(spots):
            work[pl.ds(x, N, stride=PITCH), :] = value[:, i * 128 : i * 128 + 128]

    loads[4].wait()
    loads[5].wait()

    @pl.loop(0, LANES // CHUNK)
    def _(c):
        parts = []
        for t in range(TILES):
            y = (c * TILES + t) * 2
            even = work[pl.ds(pl.multiple_of(y * PITCH, 8), N), :]
            odd = work[pl.ds(pl.multiple_of(y * PITCH + PITCH, 8), N), :]
            parts.append(jnp.concatenate([even, odd], axis=1))
        done_z = right_dot(jnp.concatenate(parts, axis=0), zb_ref)
        wide = jnp.concatenate([done_z[t * N : t * N + N] for t in range(TILES)], axis=1)
        pot = left_dot(xb_ref[:, : 3 * N], wide)
        for t in range(TILES):
            tile = c * TILES + t
            at = pl.ds(pl.multiple_of(tile * 128, 128), 128)
            below, above = visiting(tile)
            field = pot[:, t * 256 : t * 256 + 128] * below
            field += pot[:, t * 256 + 128 : t * 256 + 256] * above
            for d in range(PAIR):
                rows = [
                    field[(h * PAIR + d) * SUB : (h * PAIR + d + 1) * SUB] for h in range(2)
                ]
                outs[d][:, at] = jnp.concatenate(rows, axis=0).astype(jnp.bfloat16)


def overlap(q_ref, orb_ref, *refs):
    parts, gram_ref, flat = refs[0:8], refs[8], refs[9]
    for d in range(PAIR):
        base = (q_ref[0] ^ d) * 2
        for i in range(2):
            at = pl.ds(pl.multiple_of((base + i) * SLAB, SLAB), SLAB)
            flat[at, :] = parts[i * PAIR + d][...]
    rows = BLK * SLAB
    high, low = split(orb_ref[...].reshape(rows, LANES))
    dims = (((1,), (1,)), ((), ()))
    cross = lax.dot_general(high, flat[...], dims, preferred_element_type=jnp.float32)
    cross += lax.dot_general(low, flat[...], dims, preferred_element_type=jnp.float32)
    down = lax.broadcasted_iota(jnp.int32, (rows, rows), 0)
    along = lax.broadcasted_iota(jnp.int32, (rows, rows), 1)
    cross = jnp.where(down % SLAB == along % SLAB, cross, 0.0)
    summed = jnp.sum(cross.reshape(BLK, SLAB, rows), axis=1)
    pick_at = lax.broadcasted_iota(jnp.int32, (rows, BLK), 0) // SLAB
    pick = (pick_at == lax.broadcasted_iota(jnp.int32, (rows, BLK), 1)).astype(jnp.float32)
    gram_ref[...] = lax.dot_general(
        summed,
        pick,
        (((1,), (0,)), ((), ())),
        precision=lax.Precision.HIGHEST,
        preferred_element_type=jnp.float32,
    ) / math.sqrt(N**3)


def widen(q_ref, *refs):
    parts, field_ref = refs[0:8], refs[8]
    for d in range(PAIR):
        base = (q_ref[0] ^ d) * 2
        for i in range(2):
            field_ref[base + i] = parts[i * PAIR + d][...].astype(jnp.float32)


PARAMS = pltpu.CompilerParams(vmem_limit_bytes=VMEM_LIMIT)
PIECE = jax.ShapeDtypeStruct((2, SLAB, LANES), jnp.bfloat16)
SENT = jax.ShapeDtypeStruct((SLAB, LANES), jnp.bfloat16)


def on_device(orbitals, pair_table, partner_offset):
    q = lax.axis_index("pair").astype(jnp.int32).reshape(1)

    def across(value, d):
        return lax.ppermute(value, "pair", [(i, i ^ d) for i in range(PAIR)])

    spread, *own = pl.pallas_call(
        arrange,
        out_shape=[jax.ShapeDtypeStruct((SPOTS, BLK * SUB, 128), jnp.bfloat16)] + [PIECE] * 4,
        in_specs=[SMEM, VMEM],
        out_specs=[VMEM] * 5,
        compiler_params=PARAMS,
        name="arrange",
    )(q, orbitals)
    own = [own[0]] + [across(own[d], d) for d in range(1, PAIR)]
    held = lax.all_to_all(spread, "band", 0, 0, tiled=True)
    routed = pl.pallas_call(
        route,
        out_shape=jax.ShapeDtypeStruct((SPOTS * PAIR, 4 * SUB, 128), jnp.bfloat16),
        grid=(STEPS,),
        in_specs=[SMEM, SMEM, VMEM],
        out_specs=pl.BlockSpec((SPOTS * PAIR // STEPS, 4 * SUB, 128), lambda i: (i, 0, 0)),
        scratch_shapes=[
            pltpu.VMEM((SPOTS * BLK * SUB, 128), jnp.float32),
            pltpu.SMEM((BLK,), jnp.int32),
            pltpu.SMEM((BLK,), jnp.int32),
        ],
        compiler_params=PARAMS,
        name="route",
    )(pair_table, partner_offset, held)
    seen = lax.all_to_all(routed, ("band", "pair"), 0, 0, tiled=True)
    consts = [jnp.asarray(t) for t in tables()]
    back = []
    for a in range(2):
        sent = pl.pallas_call(
            functools.partial(solve, a),
            out_shape=[SENT] * 4,
            in_specs=[SMEM] + [VMEM] * 5 + [HBM] * 2,
            out_specs=[VMEM] * 4,
            scratch_shapes=[pltpu.VMEM((N * PITCH, 128), jnp.float32)]
            + [
                pltpu.VMEM((rows, 4 * N), jnp.bfloat16) if rows else pltpu.VMEM((N, N, 2 * N), jnp.float32)
                for rows in (N, 8 * N, N, 0, 8 * N, N)
            ]
            + [pltpu.SemaphoreType.DMA((6,))],
            compiler_params=pltpu.CompilerParams(vmem_limit_bytes=50 * 1024 * 1024),
            cost_estimate=pl.CostEstimate(
                flops=10_000_000_000, bytes_accessed=8_000_000, transcendentals=0
            ),
            name="solve",
        )(q, *own, seen, *consts)
        back += [sent[0]] + [across(sent[d], d) for d in range(1, PAIR)]
    gram = pl.pallas_call(
        overlap,
        out_shape=jax.ShapeDtypeStruct((BLK, BLK), jnp.float32),
        in_specs=[SMEM] + [VMEM] * 9,
        out_specs=VMEM,
        scratch_shapes=[pltpu.VMEM((BLK * SLAB, LANES), jnp.bfloat16)],
        compiler_params=PARAMS,
        name="overlap",
    )(q, orbitals, *back)
    others = [across(gram, d) for d in range(1, PAIR)]
    field = pl.pallas_call(
        widen,
        out_shape=jax.ShapeDtypeStruct((BLK, SLAB, LANES), jnp.float32),
        in_specs=[SMEM] + [VMEM] * 8,
        out_specs=VMEM,
        compiler_params=PARAMS,
        cost_estimate=pl.CostEstimate(flops=0, bytes_accessed=8_000_000, transcendentals=0),
        name="widen",
    )(q, *back)
    return field, (gram + others[0]) + (others[1] + others[2])


def solution(mesh):
    return jax.shard_map(
        on_device,
        mesh=mesh,
        in_specs=(P("band", "pair", None), P(), P()),
        out_specs=(P("band", "pair", None), P("band", None)),
        check_vma=False,
    )
```

```python
import functools
import math

import jax
import jax.numpy as jnp
import ml_dtypes
import numpy as np
from jax import lax
from jax.experimental import pallas as pl
from jax.experimental.pallas import tpu as pltpu
from jax.sharding import PartitionSpec as P

N = 64
BLK = 8
PAIR = 4
SLAB = 16
LANES = 4096
SCREEN = 0.0025
TILES = 32
CHUNK = TILES * 128
XSTEP = 32
PITCH = 72
SUB = 8
SPOTS = 64
STEPS = 4
X_FORWARD = 0
X_BACK = 256
Z_BOTH = 512
Y_BOTH = 768
ROWS = 832
VMEM_LIMIT = 48 * 1024 * 1024

VMEM = pl.BlockSpec(memory_space=pltpu.VMEM)
SMEM = pl.BlockSpec(memory_space=pltpu.SMEM)
HBM = pl.BlockSpec(memory_space=pltpu.HBM)


def cas_matrix():
    products = np.outer(np.arange(N), np.arange(N)) % N
    angles = 2.0 * math.pi / N * products
    return np.cos(angles) + np.sin(angles)


def halves(matrix):
    high = matrix.astype(ml_dtypes.bfloat16)
    low = (matrix - high.astype(np.float64)).astype(ml_dtypes.bfloat16)
    return high, low


def three(matrix):
    high, low = halves(matrix)
    return np.concatenate([high, high, low], axis=-1)


def tables():
    cas = cas_matrix()
    order = np.array(
        [
            [(q ^ d) * SLAB + h * SUB + r for h in range(2) for d in range(PAIR) for r in range(SUB)]
            for q in range(PAIR)
        ]
    )
    x_forward = np.stack([three(cas[:, order[q]]) for q in range(PAIR)])
    x_back = np.stack([three(cas[order[q], :]) for q in range(PAIR)])
    y_both = three(cas)
    pair = np.zeros((2 * N, 2 * N))
    pair[:N, :N] = pair[N:, N:] = cas
    high, low = halves(pair)
    z_both = np.block([[high, low], [high, np.zeros_like(low)]])
    squares = 4.0 * np.sin(math.pi * np.arange(N) / N) ** 2
    plane = squares[:, None] + squares[None, :] + SCREEN
    plane = np.concatenate([plane, plane], axis=1)
    kernel = np.concatenate([plane, np.repeat(squares[:, None], 2 * N, axis=1)])
    kernel = (kernel * N**3).astype(np.float32)
    packed = np.zeros((ROWS, 4 * N), ml_dtypes.bfloat16)
    packed[X_FORWARD : X_FORWARD + PAIR * N, : 3 * N] = x_forward.reshape(PAIR * N, 3 * N)
    packed[X_BACK : X_BACK + PAIR * N, : 3 * N] = x_back.reshape(PAIR * N, 3 * N)
    packed[Z_BOTH : Z_BOTH + 4 * N] = z_both
    packed[Y_BOTH : Y_BOTH + N, : 3 * N] = y_both
    return packed, kernel


def arrange(q_ref, orb_ref, spread_ref, *own):
    for t in range(LANES // 128):
        part = orb_ref[:, :, t * 128 : t * 128 + 128]
        for h in range(2):
            rows = part[:, h * SUB : h * SUB + SUB, :].reshape(BLK * SUB, 128)
            spread_ref[t * 2 + h] = rows.astype(jnp.bfloat16)
    for d in range(PAIR):
        base = (q_ref[0] ^ d) * 2
        for i in range(2):
            own[d][i] = orb_ref[base + i].astype(jnp.bfloat16)


def route(table_ref, offset_ref, held_ref, out_ref, wide, give_ref, take_ref):
    for p in range(BLK):
        first = table_ref[p, 0]
        second = table_ref[p, 1]
        give_ref[first] = second
        take_ref[second] = first

    gives = [give_ref[band] * SUB for band in range(BLK)]
    takes = [take_ref[band] * SUB for band in range(BLK)]
    offset = offset_ref[0]

    def picked(start):
        return wide[pl.ds(pl.multiple_of(start, SUB), SUB), :]

    @pl.when(pl.program_id(0) == 0)
    def _():
        @pl.loop(0, SPOTS, unroll=4)
        def _(j):
            at = pl.ds(pl.multiple_of(j * BLK * SUB, BLK * SUB), BLK * SUB)
            wide[at, :] = held_ref[j].astype(jnp.float32)

    @pl.loop(0, SPOTS // STEPS, unroll=4)
    def _(at):
        b = pl.program_id(0) * (SPOTS // STEPS) + at
        below = ((b - offset) & (SPOTS - 1)) * (BLK * SUB)
        above = ((b + offset) & (SPOTS - 1)) * (BLK * SUB)
        for q in range(PAIR):
            rows = []
            for band in (q * 2, q * 2 + 1):
                rows += [picked(below + gives[band]), picked(above + takes[band])]
            out_ref[at * PAIR + q] = jnp.concatenate(rows, axis=0).astype(jnp.bfloat16)


def split(value):
    high = value.astype(jnp.bfloat16)
    low = (value - high.astype(jnp.float32)).astype(jnp.bfloat16)
    return high, low


def left_dot(table, value):
    high, low = split(value)
    stacked = jnp.concatenate([high, low, high], axis=0)
    return jnp.dot(table, stacked, preferred_element_type=jnp.float32)


def right_dot(value, table):
    out = jnp.dot(
        jnp.concatenate(split(value), axis=1), table, preferred_element_type=jnp.float32
    )
    return out[:, : 2 * N] + out[:, 2 * N :]


def woven(first, second):
    left = lax.broadcasted_iota(jnp.int32, first.shape, 1) < N
    return (
        jnp.where(left, first, pltpu.roll(second, N, 1)),
        jnp.where(left, pltpu.roll(first, N, 1), second),
    )


def solve(a, q_ref, *refs):
    own, seen = refs[0:4], refs[4]
    packed, kernel, outs, work = refs[5], refs[6], refs[7:11], refs[11]
    xf_ref, z_ref, y_ref, k_ref, xb_ref = rooms = refs[12:17]
    sems = refs[17]
    q = q_ref[0]
    cast = jnp.float32
    here = pl.multiple_of(q * N, N)
    sources = (
        packed.at[pl.ds(X_FORWARD + here, N)],
        packed.at[pl.ds(Z_BOTH, 4 * N)],
        packed.at[pl.ds(Y_BOTH, N)],
        kernel,
        packed.at[pl.ds(X_BACK + here, N)],
    )
    loads = [
        pltpu.make_async_copy(source, room, sems.at[n])
        for n, (source, room) in enumerate(zip(sources, rooms))
    ]
    for load in loads:
        load.start()
    rows_at = slice(a * 2 * SUB, (a + 1) * 2 * SUB)

    def visiting(tile):
        below, above = [], []
        for h in range(2):
            for d in range(PAIR):
                rows = seen[(tile * 2 + h) * PAIR + (q ^ d), rows_at].astype(cast)
                below.append(rows[:SUB])
                above.append(rows[SUB:])
        return jnp.concatenate(below, axis=0), jnp.concatenate(above, axis=0)

    loads[0].wait()
    loads[1].wait()

    @pl.loop(0, LANES // CHUNK)
    def _(c):
        wide = []
        for t in range(TILES):
            tile = c * TILES + t
            at = pl.ds(pl.multiple_of(tile * 128, 128), 128)
            slabs = [own[d][a, :, at].astype(cast) for d in range(PAIR)]
            mine = jnp.concatenate(
                [slabs[d][h * SUB : h * SUB + SUB] for h in range(2) for d in range(PAIR)], axis=0
            )
            below, above = visiting(tile)
            wide += [mine * below, mine * above]
        done_x = left_dot(xf_ref[:, : 3 * N], jnp.concatenate(wide, axis=1))
        tall = jnp.concatenate(
            [done_x[:, t * 128 : t * 128 + 128] for t in range(2 * TILES)], axis=0
        )
        done_z = right_dot(tall, z_ref[...])
        for t in range(TILES):
            part = done_z[t * 2 * N : (t + 1) * 2 * N]
            even, odd = woven(part[:N], part[N:])
            y = (c * TILES + t) * 2
            work[pl.ds(pl.multiple_of(y * PITCH, 8), N), :] = even
            work[pl.ds(pl.multiple_of(y * PITCH + PITCH, 8), N), :] = odd

    loads[2].wait()
    loads[3].wait()

    @pl.loop(0, N // XSTEP)
    def _(step):
        spots = [step * XSTEP + i for i in range(XSTEP)]
        value = jnp.concatenate([work[pl.ds(x, N, stride=PITCH), :] for x in spots], axis=1)
        value = left_dot(y_ref[:, : 3 * N], value)
        plane = k_ref[:N]
        level = [1.0 / (plane + k_ref[pl.ds(N + x, 1), :]) for x in spots]
        value = left_dot(y_ref[:, : 3 * N], value * jnp.concatenate(level, axis=1))
        for i, x in enumerate(spots):
            work[pl.ds(x, N, stride=PITCH), :] = value[:, i * 128 : i * 128 + 128]

    loads[4].wait()

    @pl.loop(0, LANES // CHUNK)
    def _(c):
        parts = []
        for t in range(TILES):
            y = (c * TILES + t) * 2
            even = work[pl.ds(pl.multiple_of(y * PITCH, 8), N), :]
            odd = work[pl.ds(pl.multiple_of(y * PITCH + PITCH, 8), N), :]
            parts += woven(even, odd)
        done_z = right_dot(jnp.concatenate(parts, axis=0), z_ref[...])
        wide = jnp.concatenate([done_z[t * N : t * N + N] for t in range(2 * TILES)], axis=1)
        pot = left_dot(xb_ref[:, : 3 * N], wide)
        for t in range(TILES):
            tile = c * TILES + t
            at = pl.ds(pl.multiple_of(tile * 128, 128), 128)
            below, above = visiting(tile)
            field = pot[:, t * 256 : t * 256 + 128] * below
            field += pot[:, t * 256 + 128 : t * 256 + 256] * above
            for d in range(PAIR):
                rows = [
                    field[(h * PAIR + d) * SUB : (h * PAIR + d + 1) * SUB] for h in range(2)
                ]
                outs[d][:, at] = jnp.concatenate(rows, axis=0).astype(jnp.bfloat16)


def overlap(q_ref, orb_ref, *refs):
    parts, gram_ref, flat = refs[0:8], refs[8], refs[9]
    for d in range(PAIR):
        base = (q_ref[0] ^ d) * 2
        for i in range(2):
            at = pl.ds(pl.multiple_of((base + i) * SLAB, SLAB), SLAB)
            flat[at, :] = parts[i * PAIR + d][...]
    rows = BLK * SLAB
    high, low = split(orb_ref[...].reshape(rows, LANES))
    dims = (((1,), (1,)), ((), ()))
    cross = lax.dot_general(high, flat[...], dims, preferred_element_type=jnp.float32)
    cross += lax.dot_general(low, flat[...], dims, preferred_element_type=jnp.float32)
    down = lax.broadcasted_iota(jnp.int32, (rows, rows), 0)
    along = lax.broadcasted_iota(jnp.int32, (rows, rows), 1)
    cross = jnp.where(down % SLAB == along % SLAB, cross, 0.0)
    summed = jnp.sum(cross.reshape(BLK, SLAB, rows), axis=1)
    pick_at = lax.broadcasted_iota(jnp.int32, (rows, BLK), 0) // SLAB
    pick = (pick_at == lax.broadcasted_iota(jnp.int32, (rows, BLK), 1)).astype(jnp.float32)
    gram_ref[...] = lax.dot_general(
        summed,
        pick,
        (((1,), (0,)), ((), ())),
        precision=lax.Precision.HIGHEST,
        preferred_element_type=jnp.float32,
    ) / math.sqrt(N**3)


def widen(q_ref, *refs):
    parts, field_ref = refs[0:8], refs[8]
    for d in range(PAIR):
        base = (q_ref[0] ^ d) * 2
        for i in range(2):
            field_ref[base + i] = parts[i * PAIR + d][...].astype(jnp.float32)


PARAMS = pltpu.CompilerParams(vmem_limit_bytes=VMEM_LIMIT)
PIECE = jax.ShapeDtypeStruct((2, SLAB, LANES), jnp.bfloat16)
SENT = jax.ShapeDtypeStruct((SLAB, LANES), jnp.bfloat16)


def on_device(orbitals, pair_table, partner_offset):
    q = lax.axis_index("pair").astype(jnp.int32).reshape(1)

    def across(value, d):
        return lax.ppermute(value, "pair", [(i, i ^ d) for i in range(PAIR)])

    spread, *own = pl.pallas_call(
        arrange,
        out_shape=[jax.ShapeDtypeStruct((SPOTS, BLK * SUB, 128), jnp.bfloat16)] + [PIECE] * 4,
        in_specs=[SMEM, VMEM],
        out_specs=[VMEM] * 5,
        compiler_params=PARAMS,
        name="arrange",
    )(q, orbitals)
    own = [own[0]] + [across(own[d], d) for d in range(1, PAIR)]
    held = lax.all_to_all(spread, "band", 0, 0, tiled=True)
    routed = pl.pallas_call(
        route,
        out_shape=jax.ShapeDtypeStruct((SPOTS * PAIR, 4 * SUB, 128), jnp.bfloat16),
        grid=(STEPS,),
        in_specs=[SMEM, SMEM, VMEM],
        out_specs=pl.BlockSpec((SPOTS * PAIR // STEPS, 4 * SUB, 128), lambda i: (i, 0, 0)),
        scratch_shapes=[
            pltpu.VMEM((SPOTS * BLK * SUB, 128), jnp.float32),
            pltpu.SMEM((BLK,), jnp.int32),
            pltpu.SMEM((BLK,), jnp.int32),
        ],
        compiler_params=PARAMS,
        name="route",
    )(pair_table, partner_offset, held)
    seen = lax.all_to_all(routed, ("band", "pair"), 0, 0, tiled=True)
    consts = [jnp.asarray(t) for t in tables()]
    back = []
    for a in range(2):
        sent = pl.pallas_call(
            functools.partial(solve, a),
            out_shape=[SENT] * 4,
            in_specs=[SMEM] + [VMEM] * 5 + [HBM] * 2,
            out_specs=[VMEM] * 4,
            scratch_shapes=[pltpu.VMEM(((N + 1) * PITCH, 128), jnp.float32)]
            + [
                pltpu.VMEM((rows, 4 * N), jnp.bfloat16) if rows else pltpu.VMEM((2 * N, 2 * N), jnp.float32)
                for rows in (N, 4 * N, N, 0, N)
            ]
            + [pltpu.SemaphoreType.DMA((5,))],
            compiler_params=pltpu.CompilerParams(vmem_limit_bytes=49 * 1024 * 1024),
            cost_estimate=pl.CostEstimate(
                flops=10_000_000_000, bytes_accessed=8_000_000, transcendentals=0
            ),
            name="solve",
        )(q, *own, seen, *consts)
        back += [sent[0]] + [across(sent[d], d) for d in range(1, PAIR)]
    gram = pl.pallas_call(
        overlap,
        out_shape=jax.ShapeDtypeStruct((BLK, BLK), jnp.float32),
        in_specs=[SMEM] + [VMEM] * 9,
        out_specs=VMEM,
        scratch_shapes=[pltpu.VMEM((BLK * SLAB, LANES), jnp.bfloat16)],
        compiler_params=PARAMS,
        name="overlap",
    )(q, orbitals, *back)
    others = [across(gram, d) for d in range(1, PAIR)]
    field = pl.pallas_call(
        widen,
        out_shape=jax.ShapeDtypeStruct((BLK, SLAB, LANES), jnp.float32),
        in_specs=[SMEM] + [VMEM] * 8,
        out_specs=VMEM,
        compiler_params=PARAMS,
        cost_estimate=pl.CostEstimate(flops=0, bytes_accessed=8_000_000, transcendentals=0),
        name="widen",
    )(q, *back)
    return field, (gram + others[0]) + (others[1] + others[2])


def solution(mesh):
    return jax.shard_map(
        on_device,
        mesh=mesh,
        in_specs=(P("band", "pair", None), P(), P()),
        out_specs=(P("band", "pair", None), P("band", None)),
        check_vma=False,
    )
```

```python
import functools
import math

import jax
import jax.numpy as jnp
import ml_dtypes
import numpy as np
from jax import lax
from jax.experimental import pallas as pl
from jax.experimental.pallas import tpu as pltpu
from jax.sharding import PartitionSpec as P

N = 64
BLK = 8
PAIR = 4
SLAB = 16
LANES = 4096
SCREEN = 0.0025
TILES = 32
CHUNK = TILES * 128
XSTEP = 32
PITCH = 72
SUB = 8
SPOTS = 64
STEPS = 4
X_FORWARD = 0
X_BACK = 256
Z_BOTH = 512
Y_BOTH = 768
ROWS = 4096
VMEM_LIMIT = 48 * 1024 * 1024

VMEM = pl.BlockSpec(memory_space=pltpu.VMEM)
SMEM = pl.BlockSpec(memory_space=pltpu.SMEM)
HBM = pl.BlockSpec(memory_space=pltpu.HBM)


def cas_matrix():
    products = np.outer(np.arange(N), np.arange(N)) % N
    angles = 2.0 * math.pi / N * products
    return np.cos(angles) + np.sin(angles)


def halves(matrix):
    high = matrix.astype(ml_dtypes.bfloat16)
    low = (matrix - high.astype(np.float64)).astype(ml_dtypes.bfloat16)
    return high, low


def three(matrix):
    high, low = halves(matrix)
    return np.concatenate([high, high, low], axis=-1)


def tables():
    cas = cas_matrix()
    order = np.array(
        [
            [(q ^ d) * SLAB + h * SUB + r for h in range(2) for d in range(PAIR) for r in range(SUB)]
            for q in range(PAIR)
        ]
    )
    x_forward = np.stack([three(cas[:, order[q]]) for q in range(PAIR)])
    x_back = np.stack([three(cas[order[q], :]) for q in range(PAIR)])
    y_both = three(cas)
    pair = np.zeros((2 * N, 2 * N))
    pair[:N, :N] = pair[N:, N:] = cas
    high, low = halves(pair)
    z_both = np.block([[high, low], [high, np.zeros_like(low)]])
    squares = 4.0 * np.sin(math.pi * np.arange(N) / N) ** 2
    plane = squares[:, None] + squares[None, :] + SCREEN
    plane = np.concatenate([plane, plane], axis=1)
    kernel = np.concatenate([plane, np.repeat(squares[:, None], 2 * N, axis=1)])
    kernel = (kernel * N**3).astype(np.float32)
    packed = np.zeros((ROWS, 4 * N), ml_dtypes.bfloat16)
    packed[X_FORWARD : X_FORWARD + PAIR * N, : 3 * N] = x_forward.reshape(PAIR * N, 3 * N)
    packed[X_BACK : X_BACK + PAIR * N, : 3 * N] = x_back.reshape(PAIR * N, 3 * N)
    packed[Z_BOTH : Z_BOTH + 4 * N] = z_both
    packed[Y_BOTH : Y_BOTH + N, : 3 * N] = y_both
    return packed, kernel


def arrange(q_ref, orb_ref, spread_ref, *own):
    for t in range(LANES // 128):
        part = orb_ref[:, :, t * 128 : t * 128 + 128]
        for h in range(2):
            rows = part[:, h * SUB : h * SUB + SUB, :].reshape(BLK * SUB, 128)
            spread_ref[t * 2 + h] = rows.astype(jnp.bfloat16)
    for d in range(PAIR):
        base = (q_ref[0] ^ d) * 2
        for i in range(2):
            own[d][i] = orb_ref[base + i].astype(jnp.bfloat16)


def route(table_ref, offset_ref, held_ref, out_ref, wide, give_ref, take_ref):
    for p in range(BLK):
        first = table_ref[p, 0]
        second = table_ref[p, 1]
        give_ref[first] = second
        take_ref[second] = first

    gives = [give_ref[band] * SUB for band in range(BLK)]
    takes = [take_ref[band] * SUB for band in range(BLK)]
    offset = offset_ref[0]

    def picked(start):
        return wide[pl.ds(pl.multiple_of(start, SUB), SUB), :]

    @pl.when(pl.program_id(0) == 0)
    def _():
        @pl.loop(0, SPOTS, unroll=4)
        def _(j):
            at = pl.ds(pl.multiple_of(j * BLK * SUB, BLK * SUB), BLK * SUB)
            wide[at, :] = held_ref[j].astype(jnp.float32)

    @pl.loop(0, SPOTS // STEPS, unroll=4)
    def _(at):
        b = pl.program_id(0) * (SPOTS // STEPS) + at
        below = ((b - offset) & (SPOTS - 1)) * (BLK * SUB)
        above = ((b + offset) & (SPOTS - 1)) * (BLK * SUB)
        for q in range(PAIR):
            rows = []
            for band in (q * 2, q * 2 + 1):
                rows += [picked(below + gives[band]), picked(above + takes[band])]
            out_ref[at * PAIR + q] = jnp.concatenate(rows, axis=0).astype(jnp.bfloat16)


def split(value):
    high = value.astype(jnp.bfloat16)
    low = (value - high.astype(jnp.float32)).astype(jnp.bfloat16)
    return high, low


def left_dot(table, value):
    high, low = split(value)
    stacked = jnp.concatenate([high, low, high], axis=0)
    return jnp.dot(table, stacked, preferred_element_type=jnp.float32)


def right_dot(value, table):
    out = jnp.dot(
        jnp.concatenate(split(value), axis=1), table, preferred_element_type=jnp.float32
    )
    return out[:, : 2 * N] + out[:, 2 * N :]


def woven(first, second):
    left = lax.broadcasted_iota(jnp.int32, first.shape, 1) < N
    return (
        jnp.where(left, first, pltpu.roll(second, N, 1)),
        jnp.where(left, pltpu.roll(first, N, 1), second),
    )


def solve(a, q_ref, *refs):
    own, seen = refs[0:4], refs[4]
    packed, kernel, outs, work = refs[5], refs[6], refs[7:11], refs[11]
    xf_ref, z_ref, y_ref, k_ref, xb_ref = rooms = refs[12:17]
    sems = refs[17]
    q = q_ref[0]
    cast = jnp.float32
    here = pl.multiple_of(q * N, N)
    sources = (
        packed.at[pl.ds(X_FORWARD + here, N)],
        packed.at[pl.ds(Z_BOTH, 4 * N)],
        packed.at[pl.ds(Y_BOTH, N)],
        kernel,
        packed.at[pl.ds(X_BACK + here, N)],
    )
    loads = [
        pltpu.make_async_copy(source, room, sems.at[n])
        for n, (source, room) in enumerate(zip(sources, rooms))
    ]
    for load in loads:
        load.start()
    rows_at = slice(a * 2 * SUB, (a + 1) * 2 * SUB)

    def visiting(tile):
        below, above = [], []
        for h in range(2):
            for d in range(PAIR):
                rows = seen[(tile * 2 + h) * PAIR + (q ^ d), rows_at].astype(cast)
                below.append(rows[:SUB])
                above.append(rows[SUB:])
        return jnp.concatenate(below, axis=0), jnp.concatenate(above, axis=0)

    loads[0].wait()
    loads[1].wait()

    @pl.loop(0, LANES // CHUNK)
    def _(c):
        wide = []
        for t in range(TILES):
            tile = c * TILES + t
            at = pl.ds(pl.multiple_of(tile * 128, 128), 128)
            slabs = [own[d][a, :, at].astype(cast) for d in range(PAIR)]
            mine = jnp.concatenate(
                [slabs[d][h * SUB : h * SUB + SUB] for h in range(2) for d in range(PAIR)], axis=0
            )
            below, above = visiting(tile)
            wide += [mine * below, mine * above]
        done_x = left_dot(xf_ref[:, : 3 * N], jnp.concatenate(wide, axis=1))
        tall = jnp.concatenate(
            [done_x[:, t * 128 : t * 128 + 128] for t in range(2 * TILES)], axis=0
        )
        done_z = right_dot(tall, z_ref[...])
        for t in range(TILES):
            part = done_z[t * 2 * N : (t + 1) * 2 * N]
            even, odd = woven(part[:N], part[N:])
            y = (c * TILES + t) * 2
            work[pl.ds(pl.multiple_of(y * PITCH, 8), N), :] = even
            work[pl.ds(pl.multiple_of(y * PITCH + PITCH, 8), N), :] = odd

    loads[2].wait()
    loads[3].wait()

    @pl.loop(0, N // XSTEP)
    def _(step):
        spots = [step * XSTEP + i for i in range(XSTEP)]
        value = jnp.concatenate([work[pl.ds(x, N, stride=PITCH), :] for x in spots], axis=1)
        value = left_dot(y_ref[:, : 3 * N], value)
        plane = k_ref[:N]
        level = [1.0 / (plane + k_ref[pl.ds(N + x, 1), :]) for x in spots]
        value = left_dot(y_ref[:, : 3 * N], value * jnp.concatenate(level, axis=1))
        for i, x in enumerate(spots):
            work[pl.ds(x, N, stride=PITCH), :] = value[:, i * 128 : i * 128 + 128]

    loads[4].wait()

    @pl.loop(0, LANES // CHUNK)
    def _(c):
        parts = []
        for t in range(TILES):
            y = (c * TILES + t) * 2
            even = work[pl.ds(pl.multiple_of(y * PITCH, 8), N), :]
            odd = work[pl.ds(pl.multiple_of(y * PITCH + PITCH, 8), N), :]
            parts += woven(even, odd)
        done_z = right_dot(jnp.concatenate(parts, axis=0), z_ref[...])
        wide = jnp.concatenate([done_z[t * N : t * N + N] for t in range(2 * TILES)], axis=1)
        pot = left_dot(xb_ref[:, : 3 * N], wide)
        for t in range(TILES):
            tile = c * TILES + t
            at = pl.ds(pl.multiple_of(tile * 128, 128), 128)
            below, above = visiting(tile)
            field = pot[:, t * 256 : t * 256 + 128] * below
            field += pot[:, t * 256 + 128 : t * 256 + 256] * above
            for d in range(PAIR):
                rows = [
                    field[(h * PAIR + d) * SUB : (h * PAIR + d + 1) * SUB] for h in range(2)
                ]
                outs[d][:, at] = jnp.concatenate(rows, axis=0).astype(jnp.bfloat16)


def overlap(q_ref, orb_ref, *refs):
    parts, gram_ref, flat = refs[0:8], refs[8], refs[9]
    for d in range(PAIR):
        base = (q_ref[0] ^ d) * 2
        for i in range(2):
            at = pl.ds(pl.multiple_of((base + i) * SLAB, SLAB), SLAB)
            flat[at, :] = parts[i * PAIR + d][...]
    rows = BLK * SLAB
    high, low = split(orb_ref[...].reshape(rows, LANES))
    dims = (((1,), (1,)), ((), ()))
    cross = lax.dot_general(high, flat[...], dims, preferred_element_type=jnp.float32)
    cross += lax.dot_general(low, flat[...], dims, preferred_element_type=jnp.float32)
    down = lax.broadcasted_iota(jnp.int32, (rows, rows), 0)
    along = lax.broadcasted_iota(jnp.int32, (rows, rows), 1)
    cross = jnp.where(down % SLAB == along % SLAB, cross, 0.0)
    summed = jnp.sum(cross.reshape(BLK, SLAB, rows), axis=1)
    pick_at = lax.broadcasted_iota(jnp.int32, (rows, BLK), 0) // SLAB
    pick = (pick_at == lax.broadcasted_iota(jnp.int32, (rows, BLK), 1)).astype(jnp.float32)
    gram_ref[...] = lax.dot_general(
        summed,
        pick,
        (((1,), (0,)), ((), ())),
        precision=lax.Precision.HIGHEST,
        preferred_element_type=jnp.float32,
    ) / math.sqrt(N**3)


def widen(q_ref, *refs):
    parts, field_ref = refs[0:8], refs[8]
    for d in range(PAIR):
        base = (q_ref[0] ^ d) * 2
        for i in range(2):
            field_ref[base + i] = parts[i * PAIR + d][...].astype(jnp.float32)


PARAMS = pltpu.CompilerParams(vmem_limit_bytes=VMEM_LIMIT)
PIECE = jax.ShapeDtypeStruct((2, SLAB, LANES), jnp.bfloat16)
SENT = jax.ShapeDtypeStruct((SLAB, LANES), jnp.bfloat16)


def on_device(orbitals, pair_table, partner_offset):
    q = lax.axis_index("pair").astype(jnp.int32).reshape(1)

    def across(value, d):
        return lax.ppermute(value, "pair", [(i, i ^ d) for i in range(PAIR)])

    spread, *own = pl.pallas_call(
        arrange,
        out_shape=[jax.ShapeDtypeStruct((SPOTS, BLK * SUB, 128), jnp.bfloat16)] + [PIECE] * 4,
        in_specs=[SMEM, VMEM],
        out_specs=[VMEM] * 5,
        compiler_params=PARAMS,
        name="arrange",
    )(q, orbitals)
    own = [own[0]] + [across(own[d], d) for d in range(1, PAIR)]
    held = lax.all_to_all(spread, "band", 0, 0, tiled=True)
    routed = pl.pallas_call(
        route,
        out_shape=jax.ShapeDtypeStruct((SPOTS * PAIR, 4 * SUB, 128), jnp.bfloat16),
        grid=(STEPS,),
        in_specs=[SMEM, SMEM, VMEM],
        out_specs=pl.BlockSpec((SPOTS * PAIR // STEPS, 4 * SUB, 128), lambda i: (i, 0, 0)),
        scratch_shapes=[
            pltpu.VMEM((SPOTS * BLK * SUB, 128), jnp.float32),
            pltpu.SMEM((BLK,), jnp.int32),
            pltpu.SMEM((BLK,), jnp.int32),
        ],
        compiler_params=PARAMS,
        name="route",
    )(pair_table, partner_offset, held)
    seen = lax.all_to_all(routed, ("band", "pair"), 0, 0, tiled=True)
    consts = [jnp.asarray(t) for t in tables()]
    back = []
    for a in range(2):
        sent = pl.pallas_call(
            functools.partial(solve, a),
            out_shape=[SENT] * 4,
            in_specs=[SMEM] + [VMEM] * 5 + [HBM] * 2,
            out_specs=[VMEM] * 4,
            scratch_shapes=[pltpu.VMEM(((N + 1) * PITCH, 128), jnp.float32)]
            + [
                pltpu.VMEM((rows, 4 * N), jnp.bfloat16) if rows else pltpu.VMEM((2 * N, 2 * N), jnp.float32)
                for rows in (N, 4 * N, N, 0, N)
            ]
            + [pltpu.SemaphoreType.DMA((5,))],
            compiler_params=pltpu.CompilerParams(vmem_limit_bytes=50 * 1024 * 1024),
            cost_estimate=pl.CostEstimate(
                flops=10_000_000_000, bytes_accessed=8_000_000, transcendentals=0
            ),
            name="solve",
        )(q, *own, seen, *consts)
        moved = {d: across(sent[d], d) for d in (3, 2, 1)}
        back += [sent[0]] + [moved[d] for d in range(1, PAIR)]
    gram = pl.pallas_call(
        overlap,
        out_shape=jax.ShapeDtypeStruct((BLK, BLK), jnp.float32),
        in_specs=[SMEM] + [VMEM] * 9,
        out_specs=VMEM,
        scratch_shapes=[pltpu.VMEM((BLK * SLAB, LANES), jnp.bfloat16)],
        compiler_params=PARAMS,
        name="overlap",
    )(q, orbitals, *back)
    others = [across(gram, d) for d in range(1, PAIR)]
    field = pl.pallas_call(
        widen,
        out_shape=jax.ShapeDtypeStruct((BLK, SLAB, LANES), jnp.float32),
        in_specs=[SMEM] + [VMEM] * 8,
        out_specs=VMEM,
        compiler_params=PARAMS,
        cost_estimate=pl.CostEstimate(flops=0, bytes_accessed=8_000_000, transcendentals=0),
        name="widen",
    )(q, *back)
    return field, (gram + others[0]) + (others[1] + others[2])


def solution(mesh):
    return jax.shard_map(
        on_device,
        mesh=mesh,
        in_specs=(P("band", "pair", None), P(), P()),
        out_specs=(P("band", "pair", None), P("band", None)),
        check_vma=False,
    )
```
